512 devices in a mesh: fsdp: 64 (over z, y), owner: 8 (over x, core).
Axes of the slice: x: 4, y: 4, z: 16, core: 2. Of those that a mesh axis runs over, the one named last changes fastest.
Arguments:
- grad: bfloat16 [256, 512, 512], P('owner', 'fsdp')
- moment: float32 [256, 512, 512], P('owner', 'fsdp'), may hold values from 0.3 to 3
- owner_table: int32 [4, 64], replicated, may hold values from 0 to 63, each once within a row
- factor_old: float32 [8, 64, 512, 512], P('owner', 'fsdp')
- root_old: bfloat16 [8, 64, 512, 512], P('owner', 'fsdp')
Outputs:
- direction: bfloat16 [256, 512, 512], P('owner', 'fsdp')
- moment_new: float32 [256, 512, 512], P('owner', 'fsdp')
- factor_new: float32 [8, 64, 512, 512], P('owner', 'fsdp')
- root_new: bfloat16 [8, 64, 512, 512], P('owner', 'fsdp')
The draws below stay inside these ranges and needn't reach their ends.
Inputs may be any that keep to these rules, and one draw needn't show every extreme that they name: `owner_table`: row c is a permutation; entry [c, f] names which of the 64 blocks of owner indices 2c and 2c + 1 (those of 2c first, 32 each) the chip at fsdp index f and owner indices 2c, 2c + 1 owns.
All inputs are finite; a program needn't handle non-finite values.
Results may differ from the reference program's by a relative error of at most 0.0057.
Values may be sent and summed in bfloat16 or wider, within the bound.
No kernel may reach another device: no remote copies, remote signals or barrier semaphores. Data moves between devices by JAX's collectives and lax.ppermute only.
A program may use at most 64 MiB of HBM per device.

```python
import math
import jax
import jax.numpy as jnp
from jax import lax

B = 512
NB = 256
N_FSDP = 64
N_OWNER = 8


def near_identity(key, shape, low, high, spread):
    key_diag, key_off = jax.random.split(key)
    diag_vals = jax.random.uniform(key_diag, shape, jnp.float32, low, high)
    off_vals = jax.random.normal(key_off, shape, jnp.float32)
    size = shape[-1]
    ident = jnp.arange(size)[:, None] == jnp.arange(size)[None, :]
    return jnp.where(ident, diag_vals, off_vals * (spread / math.sqrt(size)))


def draw_grad(key, part):
    key = jax.random.fold_in(key, 11)
    key_base, key_rows, key_cols = jax.random.split(key, 3)
    low = math.log(0.316)
    high = math.log(3.16)
    row_scale = jnp.exp(jax.random.uniform(key_rows, (NB, B, 1), jnp.float32, low, high))
    col_scale = jnp.exp(jax.random.uniform(key_cols, (NB, 1, B), jnp.float32, low, high))
    trend = jnp.sqrt(1.0 + 2.0 * jnp.arange(B, dtype=jnp.float32) / B)[None, :, None]
    base = jax.random.normal(key_base, (NB, B, B), jnp.float32)
    return (base * trend * row_scale * col_scale).astype(jnp.bfloat16)


def draw_factor_old(key, part):
    key = jax.random.fold_in(key, 12)
    values = near_identity(key, (N_OWNER, N_FSDP, B, B), 0.6, 1.0, 0.2)
    return values.astype(jnp.float32)


def draw_root_old(key, part):
    key = jax.random.fold_in(key, 13)
    values = near_identity(key, (N_OWNER, N_FSDP, B, B), 0.85, 1.15, 0.2)
    return values.astype(jnp.bfloat16)


def steps_of(rng, dims, shards, low, top_value):
    factor_of = 1.0
    for dim, shards_of in shards:
        heights = jax.random.uniform(jax.random.fold_in(jax.random.fold_in(rng, 6), dim), (shards_of,), jnp.float32, low / len(shards), top_value / len(shards))
        factor_of = factor_of * jnp.repeat(jnp.exp(heights), dims[dim] // shards_of).reshape((-1,) + (1,) * (len(dims) - 1 - dim))
    return factor_of


def setup_inputs(seed: int = 0) -> dict:
    streams_of = jax.random.split(jax.random.key(seed), 6)
    return {
        "grad": draw_grad(jax.random.fold_in(streams_of[5], 71), 0),
        "moment": jnp.clip(jnp.exp(math.log(3.0) - 2.3025851 * jax.random.uniform(streams_of[1], (NB, B, B), jnp.float32) ** steps_of(streams_of[1], (NB, B, B), ((0, 8), (1, 64)), -0.2, 0.2)), 0.3, 3.0),
        "owner_table": jax.vmap(lambda own: jax.random.permutation(own, N_FSDP))(jax.random.split(streams_of[2], (N_OWNER // 2))).reshape((N_OWNER // 2, N_FSDP)).astype(jnp.int32),
        "factor_old": draw_factor_old(jax.random.fold_in(streams_of[5], 71), 0),
        "root_old": draw_root_old(jax.random.fold_in(streams_of[5], 71), 0),
    }


def newton_step(root, factor):
    highest = lax.Precision.HIGHEST
    xmat = root.astype(jnp.float32)
    square = jnp.dot(xmat, xmat, precision=highest)
    fourth = jnp.dot(square, square, precision=highest)
    product = jnp.dot(fourth, factor, precision=highest)
    ident = jnp.eye(product.shape[0], dtype=jnp.float32)
    return (jnp.dot(xmat, 5.0 * ident - product, precision=highest) * 0.25).astype(jnp.bfloat16)

def reference(grad, moment, owner_table, factor_old, root_old):
    g_full = grad.astype(jnp.float32)
    moment_new = 0.99 * moment + 0.01 * g_full * g_full
    adam = g_full / (jnp.sqrt(moment_new) + 1e-08)
    adam_sq = lax.optimization_barrier(jnp.sum(adam * adam, axis=(1, 2)))
    chips = N_OWNER // 2
    kvec = (jnp.arange(chips, dtype=jnp.int32)[:, None] * N_FSDP + owner_table.astype(jnp.int32)).reshape(-1)

    def one_pair(index):
        block_id = kvec[index]
        chip = index // N_FSDP
        fpos = index % N_FSDP
        block = lax.dynamic_index_in_dim(grad, block_id, 0, keepdims=False)
        left = factor_old[2 * chip, fpos]
        right = factor_old[2 * chip + 1, fpos]
        left_root = root_old[2 * chip, fpos]
        right_root = root_old[2 * chip + 1, fpos]
        gram_left = lax.dot_general(block, block, (((1,), (1,)), ((), ())), preferred_element_type=jnp.float32)
        gram_right = lax.dot_general(block, block, (((0,), (0,)), ((), ())), preferred_element_type=jnp.float32)
        left_new = 0.9 * left + 0.1 / B * gram_left
        right_new = 0.9 * right + 0.1 / B * gram_right
        shampoo_left = jnp.dot(left_root, block, preferred_element_type=jnp.float32).astype(jnp.bfloat16)
        precond = jnp.dot(shampoo_left, right_root, preferred_element_type=jnp.float32).astype(jnp.bfloat16)
        return (left_new, right_new, newton_step(left_root, left_new), newton_step(right_root, right_new), precond)
    lefts, rights, left_roots, right_roots, by_pair = lax.map(one_pair, jnp.arange(NB, dtype=jnp.int32))
    precond = jnp.zeros((NB, B, B), jnp.bfloat16).at[kvec].set(by_pair)
    p_full = precond.astype(jnp.float32)
    dir_sq = lax.optimization_barrier(jnp.sum(p_full * p_full, axis=(1, 2)))
    direction = (p_full * jnp.sqrt(adam_sq / (dir_sq + 1e-06))[:, None, None]).astype(jnp.bfloat16)
    factor_new = jnp.stack([lefts.reshape(chips, N_FSDP, B, B), rights.reshape(chips, N_FSDP, B, B)], axis=1).reshape(N_OWNER, N_FSDP, B, B)
    root_new = jnp.stack([left_roots.reshape(chips, N_FSDP, B, B), right_roots.reshape(chips, N_FSDP, B, B)], axis=1).reshape(N_OWNER, N_FSDP, B, B)
    return (direction, moment_new, factor_new, root_new)
```

```python
import jax
import jax.numpy as jnp
from jax import lax
from jax.experimental import pallas as pl
from jax.experimental.pallas import tpu as pltpu
from jax.sharding import PartitionSpec as P

BF16 = jnp.bfloat16
F32 = jnp.float32
SMEM = pl.BlockSpec(memory_space=pltpu.SMEM)
VMEM = pl.BlockSpec(memory_space=pltpu.VMEM)


def swap_cores(value):
    pairs = [(source, source ^ 1) for source in range(lax.axis_size("owner"))]
    return lax.ppermute(value, "owner", pairs)


def to_fsdp(value):
    return lax.all_to_all(value, "fsdp", split_axis=0, concat_axis=0, tiled=True)


def cost(flops, nbytes):
    return pl.CostEstimate(flops=flops, bytes_accessed=nbytes, transcendentals=0)


def adam_kernel(grad_ref, moment_ref, moment_new_ref, sums_ref):
    g_full = grad_ref[...].astype(F32)
    moment_new = 0.99 * moment_ref[...] + 0.01 * g_full * g_full
    moment_new_ref[...] = moment_new
    adam = g_full / (jnp.sqrt(moment_new) + 1e-08)
    squares = adam * adam
    lanes = sum(squares[:, :, at : at + 128] for at in range(0, squares.shape[2], 128))
    sums_ref[...] = jnp.sum(lanes, axis=1)


def adam_step(grad, moment):
    blocks, rows, width = grad.shape
    step = 8
    whole = pl.BlockSpec((step, rows, width), lambda i: (i, 0, 0))
    return pl.pallas_call(
        adam_kernel,
        grid=(blocks // step,),
        in_specs=[whole, whole],
        out_specs=[whole, pl.BlockSpec((step, 128), lambda i: (i, 0))],
        out_shape=[
            jax.ShapeDtypeStruct(grad.shape, F32),
            jax.ShapeDtypeStruct((blocks, 128), F32),
        ],
        cost_estimate=cost(10 * grad.size, 10 * grad.size),
    )(grad, moment)


def pack_kernel(place_ref, grad_ref, other_ref, sums_ref, out_ref):
    count = out_ref.shape[0]
    blocks, rows, width = grad_ref.shape
    half = width // 2
    pairs = rows // 2
    side = place_ref[count]
    first = pl.multiple_of(side * half, half)
    row = lax.broadcasted_iota(jnp.int32, (2, 128), 0)

    def body(index, carry):
        owned = place_ref[index]
        local = lax.rem(owned, blocks)
        mine = lax.div(owned, blocks) == side
        for lane in range(half // 128):
            columns = pl.ds(first + lane * 128, 128)
            value = jnp.where(mine, grad_ref[local, :, columns], other_ref[local, :, columns])
            out_ref[index, pl.ds(lane * pairs, pairs)] = value.reshape(pairs, 2, 128)
        total = jnp.where(mine, sums_ref[pl.ds(local, 1), :], 0.0)
        high = total.astype(BF16).astype(F32)
        out_ref[index, out_ref.shape[1] - 1] = jnp.where(row == 0, high, total - high).astype(BF16)
        return carry

    lax.fori_loop(0, count, body, 0, unroll=4)


def pack(place, grad, other, sums):
    blocks, rows, width = grad.shape
    slabs = rows * width // 2 // 256
    return pl.pallas_call(
        pack_kernel,
        in_specs=[SMEM, VMEM, VMEM, VMEM],
        out_specs=VMEM,
        out_shape=jax.ShapeDtypeStruct((place.size - 1, slabs + 1, 2, 128), BF16),
        cost_estimate=cost(grad.size, 6 * grad.size),
    )(place, grad, other, sums)


def precondition_kernel(place_ref, mine_ref, other_ref, root_ref, root_other_ref, out_ref, block_ref):
    count, slabs, _, _ = mine_ref.shape
    _, rows, width = block_ref.shape
    half = width // 2
    pairs = rows // 2
    side = place_ref[count]
    first = pl.multiple_of(side * half, half)
    second = pl.multiple_of((1 - side) * half, half)

    def body(index, carry):
        for source, start in ((mine_ref, first), (other_ref, second)):
            for lane in range(half // 128):
                slab = source[index, pl.ds(lane * pairs, pairs)]
                block_ref[index, :, pl.ds(start + lane * 128, 128)] = slab.reshape(rows, 128)
        return carry

    lax.fori_loop(0, count, body, 0, unroll=4)
    sums = mine_ref[:, slabs - 1].astype(F32) + other_ref[:, slabs - 1].astype(F32)
    adam_sq = jnp.sum(sums)

    def products(left_ref, right_ref, start):
        block = block_ref[...].reshape(count * rows, width)
        shampoo = jnp.dot(left_ref[...], block, preferred_element_type=F32).astype(BF16)
        precond = jnp.dot(shampoo, right_ref[...], preferred_element_type=F32).astype(BF16)
        p_full = precond.astype(F32)
        dir_sq = jnp.sum(p_full * p_full)
        scale = jnp.sqrt(jnp.full((1, half), adam_sq) / (dir_sq + 1e-06))
        scaled = (p_full[:, start : start + half] * scale).astype(BF16)
        out_ref[...] = scaled.reshape(count, rows, half)

    @pl.when(side == 0)
    def _():
        products(root_ref, root_other_ref, 0)

    @pl.when(side == 1)
    def _():
        products(root_other_ref, root_ref, half)


def precondition(place, mine, other, root, root_other, rows):
    count = mine.shape[0]
    width = root.shape[0]
    return pl.pallas_call(
        precondition_kernel,
        in_specs=[SMEM, VMEM, VMEM, VMEM, VMEM],
        out_specs=[VMEM, VMEM],
        out_shape=[
            jax.ShapeDtypeStruct((count, rows, width // 2), BF16),
            jax.ShapeDtypeStruct((count, rows, width), BF16),
        ],
        cost_estimate=cost(4 * width**3, 10 * width**2),
    )(place, mine, other, root, root_other)


def unpack_kernel(place_ref, mine_ref, other_ref, out_ref):
    count, _, half = mine_ref.shape
    blocks = out_ref.shape[0]
    side = place_ref[count]
    first = pl.multiple_of(side * half, half)
    second = pl.multiple_of((1 - side) * half, half)

    def body(index, carry):
        owned = place_ref[index]
        local = lax.rem(owned, blocks)

        @pl.when(lax.div(owned, blocks) == side)
        def _():
            out_ref[local, :, pl.ds(first, half)] = mine_ref[index]
            out_ref[local, :, pl.ds(second, half)] = other_ref[index]

        return carry

    lax.fori_loop(0, count, body, 0, unroll=4)


def unpack(place, mine, other, blocks):
    _, rows, half = mine.shape
    return pl.pallas_call(
        unpack_kernel,
        in_specs=[SMEM, VMEM, VMEM],
        out_specs=VMEM,
        out_shape=jax.ShapeDtypeStruct((blocks, rows, 2 * half), BF16),
        cost_estimate=cost(mine.size, 6 * mine.size),
    )(place, mine, other)


def gram_left(values):
    return lax.dot_general(values, values, (((1,), (1,)), ((), ())), preferred_element_type=F32)


def gram_right(values):
    return lax.dot_general(values, values, (((0,), (0,)), ((), ())), preferred_element_type=F32)


def on_device(grad, moment, owner_table, factor_old, root_old):
    highest = lax.Precision.HIGHEST
    blocks, rows, width = grad.shape
    owner_pos = lax.axis_index("owner")
    side = owner_pos % 2
    place = jnp.concatenate([owner_table[owner_pos // 2], side[None]])

    other_grad = swap_cores(grad)
    moment_new, sums = adam_step(grad, moment)
    payload = pack(place, grad, other_grad, sums)
    payload, root = lax.optimization_barrier((payload, root_old[0, 0]))
    arrived = to_fsdp(payload)

    root_other = swap_cores(root)
    xmat = root.astype(F32)
    square = jnp.dot(xmat, xmat, precision=highest)
    fourth = jnp.dot(square, square, precision=highest)
    arrived, fourth, root_other = lax.optimization_barrier((arrived, fourth, root_other))

    partner = swap_cores(arrived)
    scaled, block = precondition(place, arrived, partner, root, root_other, rows)
    scaled, block, fourth = lax.optimization_barrier((scaled, block, fourth))
    back = to_fsdp(scaled)

    gram = lax.cond(side == 0, gram_left, gram_right, block.reshape(width, width))
    factor_new = 0.9 * factor_old[0, 0] + 0.1 / width * gram
    product = jnp.dot(fourth, factor_new, precision=highest)
    ident = jnp.eye(width, dtype=F32)
    root_new = (jnp.dot(xmat, 5.0 * ident - product, precision=highest) * 0.25).astype(BF16)
    back, factor_new, root_new = lax.optimization_barrier((back, factor_new, root_new))

    direction = unpack(place, back, swap_cores(back), blocks)
    return (direction, moment_new, factor_new[None, None], root_new[None, None])


def solution(mesh):
    in_specs = (
        P("owner", "fsdp", None),
        P("owner", "fsdp", None),
        P(),
        P("owner", "fsdp", None, None),
        P("owner", "fsdp", None, None),
    )
    out_specs = (
        P("owner", "fsdp", None),
        P("owner", "fsdp", None),
        P("owner", "fsdp", None, None),
        P("owner", "fsdp", None, None),
    )
    return jax.shard_map(
        on_device, mesh=mesh, in_specs=in_specs, out_specs=out_specs, check_vma=False
    )
```

```python
import jax
import jax.numpy as jnp
from jax import lax
from jax.experimental import pallas as pl
from jax.experimental.pallas import tpu as pltpu
from jax.sharding import PartitionSpec as P

BF16 = jnp.bfloat16
F32 = jnp.float32
SMEM = pl.BlockSpec(memory_space=pltpu.SMEM)
VMEM = pl.BlockSpec(memory_space=pltpu.VMEM)


def swap_cores(value):
    pairs = [(source, source ^ 1) for source in range(lax.axis_size("owner"))]
    return lax.ppermute(value, "owner", pairs)


def to_fsdp(value):
    return lax.all_to_all(value, "fsdp", split_axis=0, concat_axis=0, tiled=True)


def shape(dims, dtype):
    return jax.ShapeDtypeStruct(dims, dtype)


def run(kernel, ins, out_shape, flops, nbytes, mib=12):
    return pl.pallas_call(
        kernel,
        in_specs=[SMEM if value.dtype == jnp.int32 else VMEM for value in ins],
        out_specs=jax.tree.map(lambda _: VMEM, out_shape),
        out_shape=out_shape,
        compiler_params=pltpu.CompilerParams(vmem_limit_bytes=mib * 2**20),
        cost_estimate=pl.CostEstimate(flops=flops, bytes_accessed=nbytes, transcendentals=0),
    )(*ins)


def place():
    position = lax.axis_index("owner")
    return lax.rem(position, 2), lax.div(position, 2)


def sums_kernel(grad_ref, moment_ref, sums_ref):
    g_full = grad_ref[...].astype(F32)
    moment_new = 0.99 * moment_ref[...] + 0.01 * g_full * g_full
    adam = g_full / (jnp.sqrt(moment_new) + 1e-08)
    squares = adam * adam
    lanes = sum(squares[:, :, at : at + 128] for at in range(0, squares.shape[2], 128))
    sums_ref[...] = jnp.sum(lanes, axis=1)


def pack_kernel(table_ref, grad_ref, other_ref, sums_ref, out_ref):
    blocks, rows, width = grad_ref.shape
    half = width // 2
    pairs = rows // 2
    side, chip = place()
    first = pl.multiple_of(side * half, half)
    row = lax.broadcasted_iota(jnp.int32, (2, 128), 0)

    def body(index, carry):
        owned = table_ref[chip, index]
        local = lax.rem(owned, blocks)
        mine = lax.div(owned, blocks) == side
        for lane in range(half // 128):
            columns = pl.ds(first + lane * 128, 128)
            value = jnp.where(mine, grad_ref[local, :, columns], other_ref[local, :, columns])
            out_ref[index, pl.ds(lane * pairs, pairs)] = value.reshape(pairs, 2, 128)
        total = jnp.where(mine, sums_ref[pl.ds(local, 1), :], 0.0)
        high = total.astype(BF16).astype(F32)
        out_ref[index, out_ref.shape[1] - 1] = jnp.where(row == 0, high, total - high).astype(BF16)
        return carry

    lax.fori_loop(0, out_ref.shape[0], body, 0, unroll=16)


def unfold(packed_ref, out_ref):
    count, rows, half = out_ref.shape
    pairs = rows // 2

    def body(index, carry):
        for lane in range(half // 128):
            slab = packed_ref[index, pl.ds(lane * pairs, pairs)]
            out_ref[index, :, lane * 128 : lane * 128 + 128] = slab.reshape(rows, 128)
        return carry

    lax.fori_loop(0, count, body, 0, unroll=16)


def tails(packed_ref):
    return jnp.sum(packed_ref[:, packed_ref.shape[1] - 1].astype(F32), axis=0)


def dot(left, right):
    return jnp.dot(left, right, preferred_element_type=F32)


def first_kernel(packed_ref, left_ref, half_ref, shampoo_ref, sums_ref):
    unfold(packed_ref, half_ref)
    sums_ref[...] = tails(packed_ref)
    values = half_ref[...].reshape(shampoo_ref.shape)
    shampoo_ref[...] = dot(left_ref[...], values).astype(BF16)


def second_kernel(packed_ref, shampoo_ref, sums_ref, left_ref, right_ref, out_ref, half_ref):
    width, half = shampoo_ref.shape
    side, _ = place()
    first = pl.multiple_of(side * half, half)
    second = pl.multiple_of((1 - side) * half, half)
    unfold(packed_ref, half_ref)
    adam_sq = jnp.sum(sums_ref[...] + tails(packed_ref))
    here = shampoo_ref[...]
    there = dot(left_ref[...], half_ref[...].reshape(width, half)).astype(BF16)

    def columns(start):
        total = dot(here, right_ref[pl.ds(first, half), pl.ds(start, half)])
        total += dot(there, right_ref[pl.ds(second, half), pl.ds(start, half)])
        return total.astype(BF16).astype(F32)

    precond = columns(first)
    remote = columns(second)
    dir_sq = jnp.sum(precond * precond + remote * remote)
    scale = jnp.sqrt(jnp.full((1, half), adam_sq) / (dir_sq + 1e-06))
    out_ref[...] = (precond * scale).astype(BF16).reshape(out_ref.shape)


def pick_kernel(table_ref, rows_ref, out_ref):
    blocks = out_ref.shape[0]
    side, chip = place()

    def body(index, carry):
        owned = table_ref[chip, index]

        @pl.when(lax.div(owned, blocks) == side)
        def _():
            out_ref[lax.rem(owned, blocks)] = rows_ref[index]

        return carry

    lax.fori_loop(0, rows_ref.shape[0], body, 0, unroll=8)


def join_kernel(table_ref, picked_ref, rows_ref, out_ref):
    blocks, _, half = picked_ref.shape
    side, chip = place()
    first = pl.multiple_of(side * half, half)
    second = pl.multiple_of((1 - side) * half, half)
    out_ref[:, :, pl.ds(first, half)] = picked_ref[...]

    def body(index, carry):
        owned = table_ref[chip, index]

        @pl.when(lax.div(owned, blocks) == side)
        def _():
            out_ref[lax.rem(owned, blocks), :, pl.ds(second, half)] = rows_ref[index]

        return carry

    lax.fori_loop(0, rows_ref.shape[0], body, 0, unroll=8)


def gram_left(values):
    return lax.dot_general(values, values, (((1,), (1,)), ((), ())), preferred_element_type=F32)


def gram_right(values):
    return lax.dot_general(values, values, (((0,), (0,)), ((), ())), preferred_element_type=F32)


def on_device(grad, moment, owner_table, factor_old, root_old):
    highest = lax.Precision.HIGHEST
    blocks, rows, width = grad.shape
    half = width // 2
    count = lax.axis_size("fsdp")
    slabs = rows * half // 256
    side = lax.axis_index("owner") % 2

    other_grad = swap_cores(grad)
    sums = run(sums_kernel, (grad, moment), shape((blocks, 128), F32), 20 * grad.size, 6 * grad.size)
    payload = run(
        pack_kernel,
        (owner_table, grad, other_grad, sums),
        shape((count, slabs + 1, 2, 128), BF16),
        grad.size,
        6 * grad.size,
    )
    payload, root, late_grad, late_moment = lax.optimization_barrier(
        (payload, root_old[0, 0], grad, moment)
    )
    arrived = to_fsdp(payload)

    root_other = swap_cores(root)
    xmat = root.astype(F32)
    square = jnp.dot(xmat, xmat, precision=highest)
    fourth = jnp.dot(square, square, precision=highest)
    left = jnp.where(side == 0, root, root_other)
    right = jnp.where(side == 0, root_other, root)
    g_full = late_grad.astype(F32)
    moment_new = 0.99 * late_moment + 0.01 * g_full * g_full
    arrived, fourth, left, right, moment_new = lax.optimization_barrier(
        (arrived, fourth, left, right, moment_new)
    )

    partner = swap_cores(arrived)
    here, shampoo, part = run(
        first_kernel,
        (arrived, left),
        [shape((count, rows, half), BF16), shape((width, half), BF16), shape((2, 128), F32)],
        width**3,
        4 * width**2,
    )
    scaled, there = run(
        second_kernel,
        (partner, shampoo, part, left, right),
        [shape((count, rows, half), BF16), shape((count, rows, half), BF16)],
        3 * width**3,
        8 * width**2,
    )
    scaled, here, there, fourth = lax.optimization_barrier((scaled, here, there, fourth))
    back = to_fsdp(scaled)

    here, there = here.reshape(width, half), there.reshape(width, half)
    block = jnp.where(
        side == 0,
        jnp.concatenate([here, there], axis=1),
        jnp.concatenate([there, here], axis=1),
    )
    gram = lax.cond(side == 0, gram_left, gram_right, block)
    factor_new = 0.9 * factor_old[0, 0] + 0.1 / width * gram
    product = jnp.dot(fourth, factor_new, precision=highest)
    ident = jnp.eye(width, dtype=F32)
    root_new = (jnp.dot(xmat, 5.0 * ident - product, precision=highest) * 0.25).astype(BF16)
    back, factor_new, root_new = lax.optimization_barrier((back, factor_new, root_new))

    back_other = swap_cores(back)
    picked = run(
        pick_kernel, (owner_table, back), shape((blocks, rows, half), BF16), 0, 4 * back.size
    )
    direction = run(
        join_kernel,
        (owner_table, picked, back_other),
        shape((blocks, rows, width), BF16),
        0,
        4 * back.size,
    )
    return (direction, moment_new, factor_new[None, None], root_new[None, None])


def solution(mesh):
    in_specs = (
        P("owner", "fsdp", None),
        P("owner", "fsdp", None),
        P(),
        P("owner", "fsdp", None, None),
        P("owner", "fsdp", None, None),
    )
    out_specs = (
        P("owner", "fsdp", None),
        P("owner", "fsdp", None),
        P("owner", "fsdp", None, None),
        P("owner", "fsdp", None, None),
    )
    return jax.shard_map(
        on_device, mesh=mesh, in_specs=in_specs, out_specs=out_specs, check_vma=False
    )
```

```python
import jax
import jax.numpy as jnp
from jax import lax
from jax.experimental import pallas as pl
from jax.experimental.pallas import tpu as pltpu
from jax.sharding import PartitionSpec as P

BF16 = jnp.bfloat16
F32 = jnp.float32
SMEM = pl.BlockSpec(memory_space=pltpu.SMEM)
VMEM = pl.BlockSpec(memory_space=pltpu.VMEM)


def swap_cores(value):
    pairs = [(source, source ^ 1) for source in range(lax.axis_size("owner"))]
    return lax.ppermute(value, "owner", pairs)


def turn(count):
    return count * 5 // 8


def to_fsdp(value):
    count = lax.axis_size("fsdp")
    group = [(turn(count) + i) % count for i in range(count)]
    return lax.all_to_all(
        value, "fsdp", split_axis=0, concat_axis=0, axis_index_groups=[group], tiled=True
    )


def at_slot(index, count):
    return lax.rem(index + turn(count), count)


def shape(dims, dtype):
    return jax.ShapeDtypeStruct(dims, dtype)


def run(kernel, ins, out_shape, flops, nbytes, in_hbm=False, out_hbm=False, scratch=()):
    anywhere = pl.BlockSpec(memory_space=pl.ANY)
    vectors = anywhere if in_hbm else VMEM
    outs = anywhere if out_hbm else VMEM
    return pl.pallas_call(
        kernel,
        in_specs=[SMEM if value.dtype == jnp.int32 else vectors for value in ins],
        out_specs=jax.tree.map(lambda _: outs, out_shape),
        out_shape=out_shape,
        scratch_shapes=scratch,
        compiler_params=pltpu.CompilerParams(vmem_limit_bytes=12 * 2**20),
        cost_estimate=pl.CostEstimate(flops=flops, bytes_accessed=nbytes, transcendentals=0),
    )(*ins)


def place():
    position = lax.axis_index("owner")
    return lax.rem(position, 2), lax.div(position, 2)


def halves(half):
    side, _ = place()
    return pl.multiple_of(side * half, half), pl.multiple_of((1 - side) * half, half)


def sums_kernel(grad_hbm, moment_hbm, sums_ref, half_ref, grad_ref, moment_ref, grad_sem, moment_sem):
    copies = [
        pltpu.make_async_copy(grad_hbm, grad_ref, grad_sem),
        pltpu.make_async_copy(moment_hbm, moment_ref, moment_sem),
    ]
    for copy in copies:
        copy.start()
    for copy in copies:
        copy.wait()
    half = half_ref.shape[2]
    first, _ = halves(half)
    half_ref[...] = grad_ref[:, :, pl.ds(first, half)]
    g_full = grad_ref[...].astype(F32)
    moment_new = 0.99 * moment_ref[...] + 0.01 * g_full * g_full
    adam = g_full / (jnp.sqrt(moment_new) + 1e-08)
    squares = adam * adam
    lanes = sum(squares[:, :, at : at + 128] for at in range(0, squares.shape[2], 128))
    sums_ref[...] = jnp.sum(lanes, axis=1)


def pack_kernel(table_ref, mine_ref, other_ref, sums_ref, out_ref):
    blocks, rows, half = mine_ref.shape
    count = out_ref.shape[0]
    pairs = rows // 2
    side, chip = place()
    first, _ = halves(half)
    row = lax.broadcasted_iota(jnp.int32, (2, 128), 0)

    def body(index, carry):
        owned = table_ref[chip, at_slot(index, count)]
        local = lax.rem(owned, blocks)
        mine = lax.div(owned, blocks) == side
        for at in range(0, half, 128):
            here = mine_ref[local, :, at : at + 128]
            there = other_ref[local, :, pl.ds(first + at, 128)]
            value = jnp.where(mine, here, there).reshape(pairs, 2, 128)
            out_ref[index, at // 128 * pairs : (at // 128 + 1) * pairs] = value
        total = jnp.where(mine, sums_ref[pl.ds(local, 1), :], 0.0)
        high = total.astype(BF16).astype(F32)
        out_ref[index, out_ref.shape[1] - 1] = jnp.where(row == 0, high, total - high).astype(BF16)
        return carry

    lax.fori_loop(0, count, body, 0, unroll=16)


def unfold(packed_ref, out_ref):
    count, rows, half = out_ref.shape
    pairs = rows // 2

    def body(index, carry):
        for lane in range(half // 128):
            slab = packed_ref[index, pl.ds(lane * pairs, pairs)]
            rows_at = at_slot(index, count)
            out_ref[rows_at, :, lane * 128 : lane * 128 + 128] = slab.reshape(rows, 128)
        return carry

    lax.fori_loop(0, count, body, 0, unroll=16)


def tails(packed_ref):
    return jnp.sum(packed_ref[:, packed_ref.shape[1] - 1].astype(F32), axis=0)


def dot(left, right):
    return jnp.dot(left, right, preferred_element_type=F32)


def first_kernel(packed_ref, left_ref, half_ref, shampoo_ref, sums_ref):
    unfold(packed_ref, half_ref)
    sums_ref[...] = tails(packed_ref)
    values = half_ref[...].reshape(shampoo_ref.shape)
    shampoo_ref[...] = dot(left_ref[...], values).astype(BF16)


def second_kernel(packed_ref, shampoo_ref, sums_ref, left_ref, right_ref, out_ref, half_ref):
    width, half = shampoo_ref.shape
    first, second = halves(half)
    unfold(packed_ref, half_ref)
    adam_sq = jnp.sum(sums_ref[...] + tails(packed_ref))
    here = shampoo_ref[...]
    there = dot(left_ref[...], half_ref[...].reshape(width, half)).astype(BF16)

    def columns(start):
        total = dot(here, right_ref[pl.ds(first, half), pl.ds(start, half)])
        total += dot(there, right_ref[pl.ds(second, half), pl.ds(start, half)])
        return total.astype(BF16).astype(F32)

    precond = columns(first)
    remote = columns(second)
    dir_sq = jnp.sum(precond * precond + remote * remote)
    scale = jnp.sqrt(jnp.full((1, half), adam_sq) / (dir_sq + 1e-06))
    scaled = (precond * scale).astype(BF16).reshape(out_ref.shape)
    count = out_ref.shape[0]
    start = turn(count)
    out_ref[: count - start] = scaled[start:]
    out_ref[count - start :] = scaled[:start]


def order_kernel(table_ref, rows_ref, out_ref):
    count = rows_ref.shape[0]
    _, chip = place()

    def body(index, carry):
        out_ref[table_ref[chip, at_slot(index, count)]] = rows_ref[index]
        return carry

    lax.fori_loop(0, count, body, 0, unroll=16)


def join_kernel(mine_ref, other_ref, out_hbm, first_sem, second_sem):
    blocks = out_hbm.shape[0]
    half = mine_ref.shape[2]
    side, _ = place()
    first, second = halves(half)
    own = pl.ds(side * blocks, blocks)
    copies = [
        pltpu.make_async_copy(mine_ref.at[own], out_hbm.at[:, :, pl.ds(first, half)], first_sem),
        pltpu.make_async_copy(other_ref.at[own], out_hbm.at[:, :, pl.ds(second, half)], second_sem),
    ]
    for copy in copies:
        copy.start()
    for copy in copies:
        copy.wait()


def gram_left(values):
    return lax.dot_general(values, values, (((1,), (1,)), ((), ())), preferred_element_type=F32)


def gram_right(values):
    return lax.dot_general(values, values, (((0,), (0,)), ((), ())), preferred_element_type=F32)


def on_device(grad, moment, owner_table, factor_old, root_old):
    highest = lax.Precision.HIGHEST
    blocks, rows, width = grad.shape
    half = width // 2
    count = lax.axis_size("fsdp")
    slabs = rows * half // 256
    side = lax.axis_index("owner") % 2

    other_grad = swap_cores(grad)
    sums, mine = run(
        sums_kernel,
        (grad, moment),
        [shape((blocks, 128), F32), shape((blocks, rows, half), BF16)],
        20 * grad.size,
        6 * grad.size,
        in_hbm=True,
        scratch=[
            pltpu.VMEM(grad.shape, BF16),
            pltpu.VMEM(moment.shape, F32),
            pltpu.SemaphoreType.DMA,
            pltpu.SemaphoreType.DMA,
        ],
    )
    payload = run(
        pack_kernel,
        (owner_table, mine, other_grad, sums),
        shape((count, slabs + 1, 2, 128), BF16),
        grad.size,
        6 * grad.size,
    )
    payload, root, late_grad, late_moment = lax.optimization_barrier(
        (payload, root_old[0, 0], grad, moment)
    )
    arrived = to_fsdp(payload)

    root_other = swap_cores(root)
    xmat = root.astype(F32)
    square = jnp.dot(xmat, xmat, precision=highest)
    fourth = jnp.dot(square, square, precision=highest)
    left = jnp.where(side == 0, root, root_other)
    right = jnp.where(side == 0, root_other, root)
    g_full = late_grad.astype(F32)
    moment_new = 0.99 * late_moment + 0.01 * g_full * g_full
    arrived, fourth, left, right, moment_new = lax.optimization_barrier(
        (arrived, fourth, left, right, moment_new)
    )

    partner = swap_cores(arrived)
    here, shampoo, part = run(
        first_kernel,
        (arrived, left),
        [shape((count, rows, half), BF16), shape((width, half), BF16), shape((2, 128), F32)],
        width**3,
        4 * width**2,
    )
    scaled, there = run(
        second_kernel,
        (partner, shampoo, part, left, right),
        [shape((count, rows, half), BF16), shape((count, rows, half), BF16)],
        3 * width**3,
        8 * width**2,
    )
    scaled, here, there, fourth = lax.optimization_barrier((scaled, here, there, fourth))
    back = to_fsdp(scaled)

    here, there = here.reshape(width, half), there.reshape(width, half)
    block = jnp.where(
        side == 0,
        jnp.concatenate([here, there], axis=1),
        jnp.concatenate([there, here], axis=1),
    )
    gram = lax.cond(side == 0, gram_left, gram_right, block)
    factor_new = 0.9 * factor_old[0, 0] + 0.1 / width * gram
    product = jnp.dot(fourth, factor_new, precision=highest)
    ident = jnp.eye(width, dtype=F32)
    root_new = (jnp.dot(xmat, 5.0 * ident - product, precision=highest) * 0.25).astype(BF16)
    back, factor_new, root_new = lax.optimization_barrier((back, factor_new, root_new))

    ordered = run(order_kernel, (owner_table, back), shape(back.shape, BF16), 0, 4 * back.size)
    direction = run(
        join_kernel,
        (ordered, swap_cores(ordered)),
        shape((blocks, rows, width), BF16),
        0,
        4 * back.size,
        out_hbm=True,
        scratch=[pltpu.SemaphoreType.DMA, pltpu.SemaphoreType.DMA],
    )
    return (direction, moment_new, factor_new[None, None], root_new[None, None])


def solution(mesh):
    in_specs = (
        P("owner", "fsdp", None),
        P("owner", "fsdp", None),
        P(),
        P("owner", "fsdp", None, None),
        P("owner", "fsdp", None, None),
    )
    out_specs = (
        P("owner", "fsdp", None),
        P("owner", "fsdp", None),
        P("owner", "fsdp", None, None),
        P("owner", "fsdp", None, None),
    )
    return jax.shard_map(
        on_device, mesh=mesh, in_specs=in_specs, out_specs=out_specs, check_vma=False
    )
```

```python
import jax
import jax.numpy as jnp
from jax import lax
from jax.experimental import pallas as pl
from jax.experimental.pallas import tpu as pltpu
from jax.sharding import PartitionSpec as P

BF16 = jnp.bfloat16
F32 = jnp.float32
SMEM = pl.BlockSpec(memory_space=pltpu.SMEM)
VMEM = pl.BlockSpec(memory_space=pltpu.VMEM)
HBM = pl.BlockSpec(memory_space=pltpu.HBM)


def swap_cores(value):
    pairs = [(source, source ^ 1) for source in range(lax.axis_size("owner"))]
    return lax.ppermute(value, "owner", pairs)


def turn(count):
    return count * 21 // 32


def turn_back(count):
    return count * 19 // 32


def to_fsdp(value, start):
    count = lax.axis_size("fsdp")
    group = [(start + i) % count for i in range(count)]
    return lax.all_to_all(
        value, "fsdp", split_axis=0, concat_axis=0, axis_index_groups=[group], tiled=True
    )


def at_slot(index, count, start):
    return lax.rem(index + start, count)


def shape(dims, dtype):
    return jax.ShapeDtypeStruct(dims, dtype)


def run(kernel, ins, out_shape, flops, nbytes, out_hbm=False, scratch=()):
    outs = HBM if out_hbm else VMEM
    return pl.pallas_call(
        kernel,
        in_specs=[SMEM if value.dtype == jnp.int32 else VMEM for value in ins],
        out_specs=jax.tree.map(lambda _: outs, out_shape),
        out_shape=out_shape,
        scratch_shapes=scratch,
        compiler_params=pltpu.CompilerParams(vmem_limit_bytes=12 * 2**20),
        cost_estimate=pl.CostEstimate(flops=flops, bytes_accessed=nbytes, transcendentals=0),
    )(*ins)


def place():
    position = lax.axis_index("owner")
    return lax.rem(position, 2), lax.div(position, 2)


def halves(half):
    side, _ = place()
    return pl.multiple_of(side * half, half), pl.multiple_of((1 - side) * half, half)


def pack_kernel(table_ref, grad_ref, other_ref, sums_ref, out_hbm, out_ref, totals_ref, sems):
    blocks, rows, width = grad_ref.shape
    half = width // 2
    count = out_ref.shape[0]
    pairs = rows // 2
    side, chip = place()
    first, _ = halves(half)
    row = lax.broadcasted_iota(jnp.int32, (2, 128), 0)
    totals_ref[...] = sum(sums_ref[:, at : at + 128] for at in range(0, width, 128))

    def body(index, carry):
        owned = table_ref[chip, at_slot(index, count, turn(count))]
        local = lax.rem(owned, blocks)
        mine = lax.div(owned, blocks) == side
        for at in range(0, half, 128):
            columns = pl.ds(first + at, 128)
            value = jnp.where(mine, grad_ref[local, :, columns], other_ref[local, :, columns])
            value = value.reshape(pairs, 2, 128)
            out_ref[index, at // 128 * pairs : (at // 128 + 1) * pairs] = value
        total = jnp.where(mine, totals_ref[pl.ds(local, 1), :], 0.0)
        high = total.astype(BF16).astype(F32)
        out_ref[index, out_ref.shape[1] - 1] = jnp.where(row == 0, high, total - high).astype(BF16)
        return carry

    parts = sems.shape[0]
    step = count // parts
    copies = []
    for part in range(parts):
        lax.fori_loop(part * step, part * step + step, body, 0, unroll=step)
        slots = pl.ds(part * step, step)
        copies.append(pltpu.make_async_copy(out_ref.at[slots], out_hbm.at[slots], sems.at[part]))
        copies[-1].start()
    for copy in copies:
        copy.wait()


def unfold(packed_ref, out_ref):
    count, rows, half = out_ref.shape
    pairs = rows // 2

    def body(index, carry):
        for lane in range(half // 128):
            slab = packed_ref[index, pl.ds(lane * pairs, pairs)]
            rows_at = at_slot(index, count, turn(count))
            out_ref[rows_at, :, lane * 128 : lane * 128 + 128] = slab.reshape(rows, 128)
        return carry

    lax.fori_loop(0, count, body, 0, unroll=16)


def tails(packed_ref):
    return jnp.sum(packed_ref[:, packed_ref.shape[1] - 1].astype(F32), axis=0)


def dot(left, right):
    return jnp.dot(left, right, preferred_element_type=F32)


def first_kernel(packed_ref, left_ref, half_ref, shampoo_ref, sums_ref):
    unfold(packed_ref, half_ref)
    sums_ref[...] = tails(packed_ref)
    values = half_ref[...].reshape(shampoo_ref.shape)
    shampoo_ref[...] = dot(left_ref[...], values).astype(BF16)


def second_kernel(packed_ref, shampoo_ref, sums_ref, left_ref, right_ref, out_ref, half_ref):
    width, half = shampoo_ref.shape
    first, second = halves(half)
    unfold(packed_ref, half_ref)
    adam_sq = jnp.sum(sums_ref[...] + tails(packed_ref))
    here = shampoo_ref[...]
    there = dot(left_ref[...], half_ref[...].reshape(width, half)).astype(BF16)

    def columns(start):
        total = dot(here, right_ref[pl.ds(first, half), pl.ds(start, half)])
        total += dot(there, right_ref[pl.ds(second, half), pl.ds(start, half)])
        return total.astype(BF16).astype(F32)

    precond = columns(first)
    remote = columns(second)
    dir_sq = jnp.sum(precond * precond + remote * remote)
    scale = jnp.sqrt(jnp.full((1, half), adam_sq) / (dir_sq + 1e-06))
    scaled = (precond * scale).astype(BF16).reshape(out_ref.shape)
    count = out_ref.shape[0]
    start = turn_back(count)
    out_ref[: count - start] = scaled[start:]
    out_ref[count - start :] = scaled[:start]


def order_kernel(table_ref, rows_ref, out_ref):
    count = rows_ref.shape[0]
    _, chip = place()

    def body(index, carry):
        owned = table_ref[chip, at_slot(index, count, turn_back(count))]
        out_ref[owned] = rows_ref[index]
        return carry

    lax.fori_loop(0, count, body, 0, unroll=16)


def join_kernel(mine_ref, other_ref, out_hbm, first_sem, second_sem):
    blocks = out_hbm.shape[0]
    half = mine_ref.shape[2]
    side, _ = place()
    first, second = halves(half)
    own = pl.ds(side * blocks, blocks)
    copies = [
        pltpu.make_async_copy(mine_ref.at[own], out_hbm.at[:, :, pl.ds(first, half)], first_sem),
        pltpu.make_async_copy(other_ref.at[own], out_hbm.at[:, :, pl.ds(second, half)], second_sem),
    ]
    for copy in copies:
        copy.start()
    for copy in copies:
        copy.wait()


def gram_left(values):
    return lax.dot_general(values, values, (((1,), (1,)), ((), ())), preferred_element_type=F32)


def gram_right(values):
    return lax.dot_general(values, values, (((0,), (0,)), ((), ())), preferred_element_type=F32)


def on_device(grad, moment, owner_table, factor_old, root_old):
    highest = lax.Precision.HIGHEST
    blocks, rows, width = grad.shape
    half = width // 2
    count = lax.axis_size("fsdp")
    slabs = rows * half // 256
    side = lax.axis_index("owner") % 2

    other_grad = swap_cores(grad)
    g_full = grad.astype(F32)
    adam = g_full / (jnp.sqrt(0.99 * moment + 0.01 * g_full * g_full) + 1e-08)
    sums = jnp.sum(adam * adam, axis=1)
    payload = run(
        pack_kernel,
        (owner_table, grad, other_grad, sums),
        shape((count, slabs + 1, 2, 128), BF16),
        grad.size,
        6 * grad.size,
        out_hbm=True,
        scratch=[
            pltpu.VMEM((count, slabs + 1, 2, 128), BF16),
            pltpu.VMEM((blocks, 128), F32),
            pltpu.SemaphoreType.DMA((4,)),
        ],
    )
    payload, root, late_grad, late_moment = lax.optimization_barrier(
        (payload, root_old[0, 0], grad, moment)
    )
    arrived = to_fsdp(payload, turn(count))

    root_other = swap_cores(root)
    xmat = root.astype(F32)
    square = jnp.dot(xmat, xmat, precision=highest)
    fourth = jnp.dot(square, square, precision=highest)
    left = jnp.where(side == 0, root, root_other)
    right = jnp.where(side == 0, root_other, root)
    g_full = late_grad.astype(F32)
    moment_new = 0.99 * late_moment + 0.01 * g_full * g_full
    arrived, fourth, left, right, moment_new = lax.optimization_barrier(
        (arrived, fourth, left, right, moment_new)
    )

    partner = swap_cores(arrived)
    here, shampoo, part = run(
        first_kernel,
        (arrived, left),
        [shape((count, rows, half), BF16), shape((width, half), BF16), shape((2, 128), F32)],
        width**3,
        4 * width**2,
    )
    scaled, there = run(
        second_kernel,
        (partner, shampoo, part, left, right),
        [shape((count, rows, half), BF16), shape((count, rows, half), BF16)],
        3 * width**3,
        8 * width**2,
    )
    scaled, here, there, fourth = lax.optimization_barrier((scaled, here, there, fourth))
    back = to_fsdp(scaled, turn_back(count))

    here, there = here.reshape(width, half), there.reshape(width, half)
    block = jnp.where(
        side == 0,
        jnp.concatenate([here, there], axis=1),
        jnp.concatenate([there, here], axis=1),
    )
    gram = lax.cond(side == 0, gram_left, gram_right, block)
    factor_new = 0.9 * factor_old[0, 0] + 0.1 / width * gram
    product = jnp.dot(fourth, factor_new, precision=highest)
    ident = jnp.eye(width, dtype=F32)
    root_new = (jnp.dot(xmat, 5.0 * ident - product, precision=highest) * 0.25).astype(BF16)
    back, factor_new, root_new = lax.optimization_barrier((back, factor_new, root_new))

    ordered = run(order_kernel, (owner_table, back), shape(back.shape, BF16), 0, 4 * back.size)
    direction = run(
        join_kernel,
        (ordered, swap_cores(ordered)),
        shape((blocks, rows, width), BF16),
        0,
        4 * back.size,
        out_hbm=True,
        scratch=[pltpu.SemaphoreType.DMA, pltpu.SemaphoreType.DMA],
    )
    return (direction, moment_new, factor_new[None, None], root_new[None, None])


def solution(mesh):
    in_specs = (
        P("owner", "fsdp", None),
        P("owner", "fsdp", None),
        P(),
        P("owner", "fsdp", None, None),
        P("owner", "fsdp", None, None),
    )
    out_specs = (
        P("owner", "fsdp", None),
        P("owner", "fsdp", None),
        P("owner", "fsdp", None, None),
        P("owner", "fsdp", None, None),
    )
    return jax.shard_map(
        on_device, mesh=mesh, in_specs=in_specs, out_specs=out_specs, check_vma=False
    )
```

```python
import jax
import jax.numpy as jnp
from jax import lax
from jax.experimental import pallas as pl
from jax.experimental.pallas import tpu as pltpu
from jax.sharding import PartitionSpec as P

BF16 = jnp.bfloat16
F32 = jnp.float32
SMEM = pl.BlockSpec(memory_space=pltpu.SMEM)
VMEM = pl.BlockSpec(memory_space=pltpu.VMEM)
HBM = pl.BlockSpec(memory_space=pltpu.HBM)


def swap_cores(value):
    pairs = [(source, source ^ 1) for source in range(lax.axis_size("owner"))]
    return lax.ppermute(value, "owner", pairs)


def turn(count):
    return count * 21 // 32


def turn_back(count):
    return count * 19 // 32


def to_fsdp(value, start):
    count = lax.axis_size("fsdp")
    group = [(start + i) % count for i in range(count)]
    return lax.all_to_all(
        value, "fsdp", split_axis=0, concat_axis=0, axis_index_groups=[group], tiled=True
    )


def at_slot(index, count, start):
    return (index + start) % count


def shape(dims, dtype):
    return jax.ShapeDtypeStruct(dims, dtype)


def run(kernel, ins, out_shape, flops, nbytes, out_hbm=False, scratch=()):
    outs = HBM if out_hbm else VMEM
    return pl.pallas_call(
        kernel,
        in_specs=[SMEM if value.dtype == jnp.int32 else VMEM for value in ins],
        out_specs=jax.tree.map(lambda _: outs, out_shape),
        out_shape=out_shape,
        scratch_shapes=scratch,
        compiler_params=pltpu.CompilerParams(vmem_limit_bytes=12 * 2**20),
        cost_estimate=pl.CostEstimate(flops=flops, bytes_accessed=nbytes, transcendentals=0),
    )(*ins)


def place():
    position = lax.axis_index("owner")
    return lax.rem(position, 2), lax.div(position, 2)


def halves(half):
    side, _ = place()
    return pl.multiple_of(side * half, half), pl.multiple_of((1 - side) * half, half)


def pack_kernel(table_ref, grad_ref, other_ref, sums_ref, out_hbm, out_ref, totals_ref, sems):
    blocks, rows, width = grad_ref.shape
    half = width // 2
    count = out_ref.shape[0]
    pairs = rows // 2
    side, chip = place()
    first, _ = halves(half)
    row = lax.broadcasted_iota(jnp.int32, (2, 128), 0)
    totals_ref[...] = sum(sums_ref[:, at : at + 128] for at in range(0, width, 128))

    def fill(index):
        owned = table_ref[chip, at_slot(index, count, turn(count))]
        local = lax.rem(owned, blocks)
        mine = lax.div(owned, blocks) == side
        for at in range(0, half, 128):
            columns = pl.ds(first + at, 128)
            value = jnp.where(mine, grad_ref[local, :, columns], other_ref[local, :, columns])
            value = value.reshape(pairs, 2, 128)
            out_ref[index, at // 128 * pairs : (at // 128 + 1) * pairs] = value
        total = jnp.where(mine, totals_ref[pl.ds(local, 1), :], 0.0)
        high = total.astype(BF16).astype(F32)
        out_ref[index, out_ref.shape[1] - 1] = jnp.where(row == 0, high, total - high).astype(BF16)

    parts = sems.shape[0]
    step = count // parts
    copies = []
    for part in range(parts):
        for index in range(part * step, part * step + step):
            fill(index)
        slots = pl.ds(part * step, step)
        copies.append(pltpu.make_async_copy(out_ref.at[slots], out_hbm.at[slots], sems.at[part]))
        copies[-1].start()
    for copy in copies:
        copy.wait()


def unfold(packed_ref, out_ref):
    count, rows, half = out_ref.shape
    pairs = rows // 2

    for index in range(count):
        for lane in range(half // 128):
            slab = packed_ref[index, lane * pairs : lane * pairs + pairs]
            rows_at = at_slot(index, count, turn(count))
            out_ref[rows_at, :, lane * 128 : lane * 128 + 128] = slab.reshape(rows, 128)


def tails(packed_ref):
    return jnp.sum(packed_ref[:, packed_ref.shape[1] - 1].astype(F32), axis=0)


def dot(left, right):
    return jnp.dot(left, right, preferred_element_type=F32)


def first_kernel(packed_ref, left_ref, half_ref, shampoo_ref, sums_ref):
    unfold(packed_ref, half_ref)
    sums_ref[...] = tails(packed_ref)
    values = half_ref[...].reshape(shampoo_ref.shape)
    shampoo_ref[...] = dot(left_ref[...], values).astype(BF16)


def second_kernel(packed_ref, shampoo_ref, sums_ref, left_ref, right_ref, out_ref, half_ref):
    width, half = shampoo_ref.shape
    first, second = halves(half)
    unfold(packed_ref, half_ref)
    adam_sq = jnp.sum(sums_ref[...] + tails(packed_ref))
    here = shampoo_ref[...]
    there = dot(left_ref[...], half_ref[...].reshape(width, half)).astype(BF16)

    def columns(start):
        total = dot(here, right_ref[pl.ds(first, half), pl.ds(start, half)])
        total += dot(there, right_ref[pl.ds(second, half), pl.ds(start, half)])
        return total.astype(BF16).astype(F32)

    precond = columns(first)
    remote = columns(second)
    dir_sq = jnp.sum(precond * precond + remote * remote)
    scale = jnp.sqrt(jnp.full((1, half), adam_sq) / (dir_sq + 1e-06))
    scaled = (precond * scale).astype(BF16).reshape(out_ref.shape)
    count = out_ref.shape[0]
    start = turn_back(count)
    out_ref[: count - start] = scaled[start:]
    out_ref[count - start :] = scaled[:start]


def order_kernel(table_ref, rows_ref, out_ref):
    count = rows_ref.shape[0]
    _, chip = place()

    for index in range(count):
        owned = table_ref[chip, at_slot(index, count, turn_back(count))]
        out_ref[owned] = rows_ref[index]


def join_kernel(mine_ref, other_ref, out_hbm, first_sem, second_sem):
    blocks = out_hbm.shape[0]
    half = mine_ref.shape[2]
    side, _ = place()
    first, second = halves(half)
    own = pl.ds(side * blocks, blocks)
    copies = [
        pltpu.make_async_copy(mine_ref.at[own], out_hbm.at[:, :, pl.ds(first, half)], first_sem),
        pltpu.make_async_copy(other_ref.at[own], out_hbm.at[:, :, pl.ds(second, half)], second_sem),
    ]
    for copy in copies:
        copy.start()
    for copy in copies:
        copy.wait()


def gram_left(values):
    return lax.dot_general(values, values, (((1,), (1,)), ((), ())), preferred_element_type=F32)


def gram_right(values):
    return lax.dot_general(values, values, (((0,), (0,)), ((), ())), preferred_element_type=F32)


def on_device(grad, moment, owner_table, factor_old, root_old):
    highest = lax.Precision.HIGHEST
    blocks, rows, width = grad.shape
    half = width // 2
    count = lax.axis_size("fsdp")
    slabs = rows * half // 256
    side = lax.axis_index("owner") % 2

    other_grad = swap_cores(grad)
    g_full = grad.astype(F32)
    adam = g_full / (jnp.sqrt(0.99 * moment + 0.01 * g_full * g_full) + 1e-08)
    sums = jnp.sum(adam * adam, axis=1)
    payload = run(
        pack_kernel,
        (owner_table, grad, other_grad, sums),
        shape((count, slabs + 1, 2, 128), BF16),
        grad.size,
        6 * grad.size,
        out_hbm=True,
        scratch=[
            pltpu.VMEM((count, slabs + 1, 2, 128), BF16),
            pltpu.VMEM((blocks, 128), F32),
            pltpu.SemaphoreType.DMA((4,)),
        ],
    )
    payload, root, late_grad, late_moment = lax.optimization_barrier(
        (payload, root_old[0, 0], grad, moment)
    )
    arrived = to_fsdp(payload, turn(count))

    root_other = swap_cores(root)
    xmat = root.astype(F32)
    square = jnp.dot(xmat, xmat, precision=highest)
    fourth = jnp.dot(square, square, precision=highest)
    left = jnp.where(side == 0, root, root_other)
    right = jnp.where(side == 0, root_other, root)
    g_full = late_grad.astype(F32)
    moment_new = 0.99 * late_moment + 0.01 * g_full * g_full
    arrived, fourth, left, right, moment_new = lax.optimization_barrier(
        (arrived, fourth, left, right, moment_new)
    )

    partner = swap_cores(arrived)
    here, shampoo, part = run(
        first_kernel,
        (arrived, left),
        [shape((count, rows, half), BF16), shape((width, half), BF16), shape((2, 128), F32)],
        width**3,
        4 * width**2,
    )
    scaled, there = run(
        second_kernel,
        (partner, shampoo, part, left, right),
        [shape((count, rows, half), BF16), shape((count, rows, half), BF16)],
        3 * width**3,
        8 * width**2,
    )
    scaled, here, there, fourth = lax.optimization_barrier((scaled, here, there, fourth))
    back = to_fsdp(scaled, turn_back(count))

    here, there = here.reshape(width, half), there.reshape(width, half)
    block = jnp.where(
        side == 0,
        jnp.concatenate([here, there], axis=1),
        jnp.concatenate([there, here], axis=1),
    )
    gram = lax.cond(side == 0, gram_left, gram_right, block)
    factor_new = 0.9 * factor_old[0, 0] + 0.1 / width * gram
    product = jnp.dot(fourth, factor_new, precision=highest)
    ident = jnp.eye(width, dtype=F32)
    root_new = (jnp.dot(xmat, 5.0 * ident - product, precision=highest) * 0.25).astype(BF16)
    back, factor_new, root_new = lax.optimization_barrier((back, factor_new, root_new))

    ordered = run(order_kernel, (owner_table, back), shape(back.shape, BF16), 0, 4 * back.size)
    direction = run(
        join_kernel,
        (ordered, swap_cores(ordered)),
        shape((blocks, rows, width), BF16),
        0,
        4 * back.size,
        out_hbm=True,
        scratch=[pltpu.SemaphoreType.DMA, pltpu.SemaphoreType.DMA],
    )
    return (direction, moment_new, factor_new[None, None], root_new[None, None])


def solution(mesh):
    in_specs = (
        P("owner", "fsdp", None),
        P("owner", "fsdp", None),
        P(),
        P("owner", "fsdp", None, None),
        P("owner", "fsdp", None, None),
    )
    out_specs = (
        P("owner", "fsdp", None),
        P("owner", "fsdp", None),
        P("owner", "fsdp", None, None),
        P("owner", "fsdp", None, None),
    )
    return jax.shard_map(
        on_device, mesh=mesh, in_specs=in_specs, out_specs=out_specs, check_vma=False
    )
```

```python
import jax
import jax.numpy as jnp
from jax import lax
from jax.experimental import pallas as pl
from jax.experimental.pallas import tpu as pltpu
from jax.sharding import PartitionSpec as P

BF16 = jnp.bfloat16
F32 = jnp.float32
SMEM = pl.BlockSpec(memory_space=pltpu.SMEM)
VMEM = pl.BlockSpec(memory_space=pltpu.VMEM)
HBM = pl.BlockSpec(memory_space=pltpu.HBM)


def swap_cores(value):
    pairs = [(source, source ^ 1) for source in range(lax.axis_size("owner"))]
    return lax.ppermute(value, "owner", pairs)


def turn(count):
    return count * 45 // 64


def turn_back(count):
    return count * 41 // 64


def to_fsdp(value, start):
    count = lax.axis_size("fsdp")
    group = [(start + i) % count for i in range(count)]
    return lax.all_to_all(
        value, "fsdp", split_axis=0, concat_axis=0, axis_index_groups=[group], tiled=True
    )


def at_slot(index, count, start):
    return (index + start) % count


def shape(dims, dtype):
    return jax.ShapeDtypeStruct(dims, dtype)


def run(kernel, ins, out_shape, flops, nbytes, out_hbm=False, scratch=()):
    outs = HBM if out_hbm else VMEM
    return pl.pallas_call(
        kernel,
        in_specs=[SMEM if value.dtype == jnp.int32 else VMEM for value in ins],
        out_specs=jax.tree.map(lambda _: outs, out_shape),
        out_shape=out_shape,
        scratch_shapes=scratch,
        compiler_params=pltpu.CompilerParams(vmem_limit_bytes=12 * 2**20),
        cost_estimate=pl.CostEstimate(flops=flops, bytes_accessed=nbytes, transcendentals=0),
    )(*ins)


def place():
    position = lax.axis_index("owner")
    return lax.rem(position, 2), lax.div(position, 2)


def halves(half):
    side, _ = place()
    return pl.multiple_of(side * half, half), pl.multiple_of((1 - side) * half, half)


def pack_kernel(table_ref, grad_ref, other_ref, sums_ref, out_hbm, out_ref, totals_ref, sems):
    blocks, rows, width = grad_ref.shape
    half = width // 2
    count = out_ref.shape[0]
    pairs = rows // 2
    side, chip = place()
    first, _ = halves(half)
    row = lax.broadcasted_iota(jnp.int32, (2, 128), 0)
    totals_ref[...] = sum(sums_ref[:, at : at + 128] for at in range(0, width, 128))

    def fill(index):
        owned = table_ref[chip, at_slot(index, count, turn(count))]
        local = lax.rem(owned, blocks)
        mine = lax.div(owned, blocks) == side
        for at in range(0, half, 128):
            columns = pl.ds(first + at, 128)
            value = jnp.where(mine, grad_ref[local, :, columns], other_ref[local, :, columns])
            value = value.reshape(pairs, 2, 128)
            out_ref[index, at // 128 * pairs : (at // 128 + 1) * pairs] = value
        total = jnp.where(mine, totals_ref[pl.ds(local, 1), :], 0.0)
        high = total.astype(BF16).astype(F32)
        out_ref[index, out_ref.shape[1] - 1] = jnp.where(row == 0, high, total - high).astype(BF16)

    parts = sems.shape[0]
    step = count // parts
    copies = []
    for part in range(parts):
        for index in range(part * step, part * step + step):
            fill(index)
        slots = pl.ds(part * step, step)
        copies.append(pltpu.make_async_copy(out_ref.at[slots], out_hbm.at[slots], sems.at[part]))
        copies[-1].start()
    for copy in copies:
        copy.wait()


def unfold(packed_ref, out_ref):
    count, rows, half = out_ref.shape
    pairs = rows // 2

    for index in range(count):
        for lane in range(half // 128):
            slab = packed_ref[index, lane * pairs : lane * pairs + pairs]
            rows_at = at_slot(index, count, turn(count))
            out_ref[rows_at, :, lane * 128 : lane * 128 + 128] = slab.reshape(rows, 128)


def tails(packed_ref):
    return jnp.sum(packed_ref[:, packed_ref.shape[1] - 1].astype(F32), axis=0)


def dot(left, right):
    return jnp.dot(left, right, preferred_element_type=F32)


def first_kernel(packed_ref, left_ref, half_ref, shampoo_ref, sums_ref):
    unfold(packed_ref, half_ref)
    sums_ref[...] = tails(packed_ref)
    values = half_ref[...].reshape(shampoo_ref.shape)
    shampoo_ref[...] = dot(left_ref[...], values).astype(BF16)


def second_kernel(packed_ref, shampoo_ref, sums_ref, left_ref, right_ref, out_ref, half_ref):
    width, half = shampoo_ref.shape
    first, second = halves(half)
    unfold(packed_ref, half_ref)
    adam_sq = jnp.sum(sums_ref[...] + tails(packed_ref))
    here = shampoo_ref[...]
    there = dot(left_ref[...], half_ref[...].reshape(width, half)).astype(BF16)

    def columns(start):
        total = dot(here, right_ref[pl.ds(first, half), pl.ds(start, half)])
        total += dot(there, right_ref[pl.ds(second, half), pl.ds(start, half)])
        return total.astype(BF16).astype(F32)

    precond = columns(first)
    remote = columns(second)
    dir_sq = jnp.sum(precond * precond + remote * remote)
    scale = jnp.sqrt(jnp.full((1, half), adam_sq) / (dir_sq + 1e-06))
    scaled = (precond * scale).astype(BF16).reshape(out_ref.shape)
    count = out_ref.shape[0]
    start = turn_back(count)
    out_ref[: count - start] = scaled[start:]
    out_ref[count - start :] = scaled[:start]


def order_kernel(table_ref, rows_ref, out_ref):
    count = rows_ref.shape[0]
    _, chip = place()

    for index in range(count):
        owned = table_ref[chip, at_slot(index, count, turn_back(count))]
        out_ref[owned] = rows_ref[index]


def join_kernel(mine_ref, other_ref, out_hbm, first_sem, second_sem):
    blocks = out_hbm.shape[0]
    half = mine_ref.shape[2]
    side, _ = place()
    first, second = halves(half)
    own = pl.ds(side * blocks, blocks)
    copies = [
        pltpu.make_async_copy(mine_ref.at[own], out_hbm.at[:, :, pl.ds(first, half)], first_sem),
        pltpu.make_async_copy(other_ref.at[own], out_hbm.at[:, :, pl.ds(second, half)], second_sem),
    ]
    for copy in copies:
        copy.start()
    for copy in copies:
        copy.wait()


def gram_left(values):
    return lax.dot_general(values, values, (((1,), (1,)), ((), ())), preferred_element_type=F32)


def gram_right(values):
    return lax.dot_general(values, values, (((0,), (0,)), ((), ())), preferred_element_type=F32)


def on_device(grad, moment, owner_table, factor_old, root_old):
    highest = lax.Precision.HIGHEST
    blocks, rows, width = grad.shape
    half = width // 2
    count = lax.axis_size("fsdp")
    slabs = rows * half // 256
    side = lax.axis_index("owner") % 2

    other_grad = swap_cores(grad)
    g_full = grad.astype(F32)
    adam = g_full / (jnp.sqrt(0.99 * moment + 0.01 * g_full * g_full) + 1e-08)
    sums = jnp.sum(adam * adam, axis=1)
    payload = run(
        pack_kernel,
        (owner_table, grad, other_grad, sums),
        shape((count, slabs + 1, 2, 128), BF16),
        grad.size,
        6 * grad.size,
        out_hbm=True,
        scratch=[
            pltpu.VMEM((count, slabs + 1, 2, 128), BF16),
            pltpu.VMEM((blocks, 128), F32),
            pltpu.SemaphoreType.DMA((4,)),
        ],
    )
    payload, root, late_grad, late_moment = lax.optimization_barrier(
        (payload, root_old[0, 0], grad, moment)
    )
    arrived = to_fsdp(payload, turn(count))

    root_other = swap_cores(root)
    xmat = root.astype(F32)
    square = jnp.dot(xmat, xmat, precision=highest)
    fourth = jnp.dot(square, square, precision=highest)
    left = jnp.where(side == 0, root, root_other)
    right = jnp.where(side == 0, root_other, root)
    g_full = late_grad.astype(F32)
    moment_new = 0.99 * late_moment + 0.01 * g_full * g_full
    arrived, fourth, left, right, moment_new = lax.optimization_barrier(
        (arrived, fourth, left, right, moment_new)
    )

    partner = swap_cores(arrived)
    here, shampoo, part = run(
        first_kernel,
        (arrived, left),
        [shape((count, rows, half), BF16), shape((width, half), BF16), shape((2, 128), F32)],
        width**3,
        4 * width**2,
    )
    scaled, there = run(
        second_kernel,
        (partner, shampoo, part, left, right),
        [shape((count, rows, half), BF16), shape((count, rows, half), BF16)],
        3 * width**3,
        8 * width**2,
    )
    scaled, here, there, fourth = lax.optimization_barrier((scaled, here, there, fourth))
    back = to_fsdp(scaled, turn_back(count))

    here, there = here.reshape(width, half), there.reshape(width, half)
    block = jnp.where(
        side == 0,
        jnp.concatenate([here, there], axis=1),
        jnp.concatenate([there, here], axis=1),
    )
    gram = lax.cond(side == 0, gram_left, gram_right, block)
    factor_new = 0.9 * factor_old[0, 0] + 0.1 / width * gram
    product = jnp.dot(fourth, factor_new, precision=highest)
    ident = jnp.eye(width, dtype=F32)
    root_new = (jnp.dot(xmat, 5.0 * ident - product, precision=highest) * 0.25).astype(BF16)
    back, factor_new, root_new = lax.optimization_barrier((back, factor_new, root_new))

    ordered = run(order_kernel, (owner_table, back), shape(back.shape, BF16), 0, 4 * back.size)
    direction = run(
        join_kernel,
        (ordered, swap_cores(ordered)),
        shape((blocks, rows, width), BF16),
        0,
        4 * back.size,
        out_hbm=True,
        scratch=[pltpu.SemaphoreType.DMA, pltpu.SemaphoreType.DMA],
    )
    return (direction, moment_new, factor_new[None, None], root_new[None, None])


def solution(mesh):
    in_specs = (
        P("owner", "fsdp", None),
        P("owner", "fsdp", None),
        P(),
        P("owner", "fsdp", None, None),
        P("owner", "fsdp", None, None),
    )
    out_specs = (
        P("owner", "fsdp", None),
        P("owner", "fsdp", None),
        P("owner", "fsdp", None, None),
        P("owner", "fsdp", None, None),
    )
    return jax.shard_map(
        on_device, mesh=mesh, in_specs=in_specs, out_specs=out_specs, check_vma=False
    )
```

```python
import jax
import jax.numpy as jnp
from jax import lax
from jax.experimental import pallas as pl
from jax.experimental.pallas import tpu as pltpu
from jax.sharding import PartitionSpec as P

BF16 = jnp.bfloat16
F32 = jnp.float32
SMEM = pl.BlockSpec(memory_space=pltpu.SMEM)
VMEM = pl.BlockSpec(memory_space=pltpu.VMEM)
HBM = pl.BlockSpec(memory_space=pltpu.HBM)


def swap_cores(value):
    pairs = [(source, source ^ 1) for source in range(lax.axis_size("owner"))]
    return lax.ppermute(value, "owner", pairs)


def turn(count):
    return count * 45 // 64


def turn_back(count):
    return count * 41 // 64


def to_fsdp(value, start):
    count = lax.axis_size("fsdp")
    group = [(start + i) % count for i in range(count)]
    return lax.all_to_all(
        value, "fsdp", split_axis=0, concat_axis=0, axis_index_groups=[group], tiled=True
    )


def at_slot(index, count, start):
    return (index + start) % count


def shape(dims, dtype):
    return jax.ShapeDtypeStruct(dims, dtype)


def run(kernel, ins, out_shape, flops, nbytes, out_hbm=False, scratch=()):
    outs = HBM if out_hbm else VMEM
    return pl.pallas_call(
        kernel,
        in_specs=[SMEM if value.dtype == jnp.int32 else VMEM for value in ins],
        out_specs=jax.tree.map(lambda _: outs, out_shape),
        out_shape=out_shape,
        scratch_shapes=scratch,
        compiler_params=pltpu.CompilerParams(vmem_limit_bytes=12 * 2**20),
        cost_estimate=pl.CostEstimate(flops=flops, bytes_accessed=nbytes, transcendentals=0),
    )(*ins)


def place():
    position = lax.axis_index("owner")
    return lax.rem(position, 2), lax.div(position, 2)


def halves(half):
    side, _ = place()
    return pl.multiple_of(side * half, half), pl.multiple_of((1 - side) * half, half)


def pack_kernel(table_ref, grad_ref, other_ref, sums_ref, out_hbm, out_ref, high_ref, low_ref, sems):
    blocks, rows, width = grad_ref.shape
    half = width // 2
    count = out_ref.shape[0]
    pairs = rows // 2
    side, chip = place()
    first, _ = halves(half)
    row = lax.broadcasted_iota(jnp.int32, (2, 128), 0)
    totals = sum(sums_ref[:, at : at + 128] for at in range(0, width, 128))
    high = totals.astype(BF16).astype(F32)
    high_ref[...] = high
    low_ref[...] = totals - high

    def fill(index):
        owned = table_ref[chip, at_slot(index, count, turn(count))]
        local = lax.rem(owned, blocks)
        mine = lax.div(owned, blocks) == side
        for at in range(0, half, 128):
            columns = pl.ds(first + at, 128)
            value = jnp.where(mine, grad_ref[local, :, columns], other_ref[local, :, columns])
            value = value.reshape(pairs, 2, 128)
            out_ref[index, at // 128 * pairs : (at // 128 + 1) * pairs] = value
        here = pl.ds(local, 1)
        total = jnp.where(row == 0, high_ref[here, :], low_ref[here, :])
        out_ref[index, out_ref.shape[1] - 1] = jnp.where(mine, total, 0.0).astype(BF16)

    parts = sems.shape[0]
    step = count // parts
    copies = []
    for part in range(parts):
        for index in range(part * step, part * step + step):
            fill(index)
        slots = pl.ds(part * step, step)
        copies.append(pltpu.make_async_copy(out_ref.at[slots], out_hbm.at[slots], sems.at[part]))
        copies[-1].start()
    for copy in copies:
        copy.wait()


def unfold(packed_ref, out_ref):
    count, rows, half = out_ref.shape
    pairs = rows // 2

    for index in range(count):
        for lane in range(half // 128):
            slab = packed_ref[index, lane * pairs : lane * pairs + pairs]
            rows_at = at_slot(index, count, turn(count))
            out_ref[rows_at, :, lane * 128 : lane * 128 + 128] = slab.reshape(rows, 128)


def tails(packed_ref):
    return jnp.sum(packed_ref[:, packed_ref.shape[1] - 1].astype(F32), axis=0)


def dot(left, right):
    return jnp.dot(left, right, preferred_element_type=F32)


def first_kernel(packed_ref, left_ref, half_ref, shampoo_ref, sums_ref):
    unfold(packed_ref, half_ref)
    sums_ref[...] = tails(packed_ref)
    values = half_ref[...].reshape(shampoo_ref.shape)
    shampoo_ref[...] = dot(left_ref[...], values).astype(BF16)


def second_kernel(packed_ref, shampoo_ref, sums_ref, left_ref, right_ref, out_ref, half_ref, all_ref):
    width, half = shampoo_ref.shape
    first, second = halves(half)
    unfold(packed_ref, half_ref)
    adam_sq = jnp.sum(sums_ref[...] + tails(packed_ref))
    all_ref[:, pl.ds(first, half)] = shampoo_ref[...]
    there = dot(left_ref[...], half_ref[...].reshape(width, half))
    all_ref[:, pl.ds(second, half)] = there.astype(BF16)

    def columns(start):
        return dot(all_ref[...], right_ref[:, pl.ds(start, half)]).astype(BF16).astype(F32)

    precond = columns(first)
    remote = columns(second)
    dir_sq = jnp.sum(precond * precond + remote * remote)
    scale = jnp.sqrt(jnp.full((1, half), adam_sq) / (dir_sq + 1e-06))
    scaled = (precond * scale).astype(BF16).reshape(out_ref.shape)
    count = out_ref.shape[0]
    start = turn_back(count)
    out_ref[: count - start] = scaled[start:]
    out_ref[count - start :] = scaled[:start]


def order_kernel(table_ref, rows_ref, out_ref):
    count = rows_ref.shape[0]
    _, chip = place()

    for index in range(count):
        owned = table_ref[chip, at_slot(index, count, turn_back(count))]
        out_ref[owned] = rows_ref[index]


def join_kernel(mine_ref, other_ref, out_hbm, first_sem, second_sem):
    blocks = out_hbm.shape[0]
    half = mine_ref.shape[2]
    side, _ = place()
    first, second = halves(half)
    own = pl.ds(side * blocks, blocks)
    copies = [
        pltpu.make_async_copy(mine_ref.at[own], out_hbm.at[:, :, pl.ds(first, half)], first_sem),
        pltpu.make_async_copy(other_ref.at[own], out_hbm.at[:, :, pl.ds(second, half)], second_sem),
    ]
    for copy in copies:
        copy.start()
    for copy in copies:
        copy.wait()


def gram_left(values):
    return lax.dot_general(values, values, (((1,), (1,)), ((), ())), preferred_element_type=F32)


def gram_right(values):
    return lax.dot_general(values, values, (((0,), (0,)), ((), ())), preferred_element_type=F32)


def on_device(grad, moment, owner_table, factor_old, root_old):
    highest = lax.Precision.HIGHEST
    blocks, rows, width = grad.shape
    half = width // 2
    count = lax.axis_size("fsdp")
    slabs = rows * half // 256
    side = lax.axis_index("owner") % 2

    other_grad = swap_cores(grad)
    g_full = grad.astype(F32)
    adam = g_full / (jnp.sqrt(0.99 * moment + 0.01 * g_full * g_full) + 1e-08)
    sums = jnp.sum(adam * adam, axis=1)
    payload = run(
        pack_kernel,
        (owner_table, grad, other_grad, sums),
        shape((count, slabs + 1, 2, 128), BF16),
        grad.size,
        6 * grad.size,
        out_hbm=True,
        scratch=[
            pltpu.VMEM((count, slabs + 1, 2, 128), BF16),
            pltpu.VMEM((blocks, 128), F32),
            pltpu.VMEM((blocks, 128), F32),
            pltpu.SemaphoreType.DMA((2,)),
        ],
    )
    payload, root, late_grad, late_moment = lax.optimization_barrier(
        (payload, root_old[0, 0], grad, moment)
    )
    arrived = to_fsdp(payload, turn(count))

    root_other = swap_cores(root)
    xmat = root.astype(F32)
    square = jnp.dot(xmat, xmat, precision=highest)
    fourth = jnp.dot(square, square, precision=highest)
    left = jnp.where(side == 0, root, root_other)
    right = jnp.where(side == 0, root_other, root)
    g_full = late_grad.astype(F32)
    moment_new = 0.99 * late_moment + 0.01 * g_full * g_full
    arrived, fourth, left, right, moment_new = lax.optimization_barrier(
        (arrived, fourth, left, right, moment_new)
    )

    partner = swap_cores(arrived)
    here, shampoo, part = run(
        first_kernel,
        (arrived, left),
        [shape((count, rows, half), BF16), shape((width, half), BF16), shape((2, 128), F32)],
        width**3,
        4 * width**2,
    )
    scaled, there = run(
        second_kernel,
        (partner, shampoo, part, left, right),
        [shape((count, rows, half), BF16), shape((count, rows, half), BF16)],
        3 * width**3,
        8 * width**2,
        scratch=[pltpu.VMEM((width, width), BF16)],
    )
    scaled, here, there, fourth = lax.optimization_barrier((scaled, here, there, fourth))
    back = to_fsdp(scaled, turn_back(count))

    here, there = here.reshape(width, half), there.reshape(width, half)
    block = jnp.where(
        side == 0,
        jnp.concatenate([here, there], axis=1),
        jnp.concatenate([there, here], axis=1),
    )
    gram = lax.cond(side == 0, gram_left, gram_right, block)
    factor_new = 0.9 * factor_old[0, 0] + 0.1 / width * gram
    product = jnp.dot(fourth, factor_new, precision=highest)
    ident = jnp.eye(width, dtype=F32)
    root_new = (jnp.dot(xmat, 5.0 * ident - product, precision=highest) * 0.25).astype(BF16)
    back, factor_new, root_new = lax.optimization_barrier((back, factor_new, root_new))

    ordered = run(order_kernel, (owner_table, back), shape(back.shape, BF16), 0, 4 * back.size)
    direction = run(
        join_kernel,
        (ordered, swap_cores(ordered)),
        shape((blocks, rows, width), BF16),
        0,
        4 * back.size,
        out_hbm=True,
        scratch=[pltpu.SemaphoreType.DMA, pltpu.SemaphoreType.DMA],
    )
    return (direction, moment_new, factor_new[None, None], root_new[None, None])


def solution(mesh):
    in_specs = (
        P("owner", "fsdp", None),
        P("owner", "fsdp", None),
        P(),
        P("owner", "fsdp", None, None),
        P("owner", "fsdp", None, None),
    )
    out_specs = (
        P("owner", "fsdp", None),
        P("owner", "fsdp", None),
        P("owner", "fsdp", None, None),
        P("owner", "fsdp", None, None),
    )
    return jax.shard_map(
        on_device, mesh=mesh, in_specs=in_specs, out_specs=out_specs, check_vma=False
    )
```
